512 devices in a mesh: box: 128 (over x, z, core), lvl: 4 (over y).
Axes of the slice: x: 4, y: 4, z: 16, core: 2. Of those that a mesh axis runs over, the one named last changes fastest.
Arguments:
- near_blocks: bfloat16 [512, 24, 256, 256], P('box', 'lvl'), may hold values from -0.375 to 0.375
- self_block: bfloat16 [512, 256, 256], P('box', 'lvl'), as said below
- basis: bfloat16 [512, 256, 256], P('box', 'lvl'), may hold values from -1.5 to 1.5
- neighbours: int32 [512, 24], P('box', 'lvl'), may hold values from -1 to 511, as said below
- counts: int32 [512], P('box'), may hold values from 128 to 256
Outputs:
- fill_blocks: bfloat16 [512, 24, 128, 256], P('box', 'lvl')
The draws below stay inside these ranges and needn't reach their ends.
Inputs may be any that keep to these rules, and one draw needn't show every extreme that they name: `neighbours`: box i is owned by index i // 4 of box. Each box lists distinct other boxes, all owned by indices at most 3 away from its own owner; slots hold -1 only for boxes owned within 3 indices of either end of the axis, and there only after the used slots run out. `self_block`: Symmetric, with a positive diagonal.
All inputs are finite; a program needn't handle non-finite values.
Results may differ from the reference program's by a relative error of at most 0.007.
Values may be sent and summed in bfloat16 or wider, within the bound.
A program may use at most 64 MiB of HBM per device.

```python
import jax
import jax.numpy as jnp
from jax import lax

LEAF = 256
RED = 128
NEAR = 24
HOPS = 3
BOX_DEV = 4
BOXES = 512
N_BOX = 128


def draw_self_block(key, part):
    box_count = BOX_DEV * N_BOX
    first_key, second_key = jax.random.split(jax.random.fold_in(key, 7))
    diagonal = jax.random.uniform(first_key, (box_count, LEAF), jnp.float32, 1.0, 4.0)
    noise = jax.random.normal(second_key, (box_count, LEAF, LEAF), jnp.float32) * (0.4 / LEAF ** 0.5)
    symmetric = (noise + jnp.swapaxes(noise, 1, 2)) * 0.5 ** 0.5
    identity = jnp.eye(LEAF, dtype=jnp.float32)
    whole = symmetric * (1.0 - identity) + diagonal[:, :, None] * identity
    return whole.astype(jnp.bfloat16)


def draw_neighbours(key, part):
    box_count = BOX_DEV * N_BOX
    window_size = (2 * HOPS + 1) * BOX_DEV
    box_ids = jnp.arange(box_count, dtype=jnp.int32)
    owner = box_ids // BOX_DEV
    candidate = (owner - HOPS)[:, None] * BOX_DEV + jnp.arange(window_size, dtype=jnp.int32)[None, :]
    usable = (candidate >= 0) & (candidate < box_count) & (candidate != box_ids[:, None])
    scores = jax.random.randint(jax.random.fold_in(key, 11), (box_count, window_size), 0, 2 ** 20, dtype=jnp.int32)
    scores = scores * window_size + jnp.arange(window_size, dtype=jnp.int32)[None, :]
    scores = jnp.where(usable, scores, 2 ** 30)
    ordering = jnp.argsort(scores, axis=1, stable=True)[:, :NEAR]
    picked = jnp.take_along_axis(candidate, ordering, axis=1)
    picked_ok = jnp.take_along_axis(usable, ordering, axis=1)
    return jnp.where(picked_ok, picked, -1).astype(jnp.int32)


def touch_ends(values, own_key, low, largest):
    dims = values.shape
    spot = [jax.random.randint(jax.random.fold_in(own_key, axis), (), 0, dims[axis]) for axis in range(len(dims))]
    values = values.at[tuple(spot)].set(low)
    longest = dims.index(max(dims))
    spot[longest] = (spot[longest] + 1) % dims[longest]
    return values.at[tuple(spot)].set(largest)


def block_scale(key, shape, pieces, smallest, top_value):
    def one(position, shards_of):
        heights = jax.random.uniform(jax.random.fold_in(jax.random.fold_in(key, 6), position), (shards_of,), jnp.float32, smallest / len(pieces), top_value / len(pieces))
        return jnp.repeat(jnp.exp(heights), shape[position] // shards_of).reshape((-1,) + (1,) * (len(shape) - position - 1))

    level = one(*pieces[0])
    for cut in pieces[1:]:
        level = level * one(*cut)
    return level


def centred(stream_key, shape, width, reach, cuts=(), kind=jnp.bfloat16):
    values = width * jax.random.normal(stream_key, shape, jnp.float32)
    if cuts:
        values = values * block_scale(stream_key, shape, cuts, -0.22, 0.18)
    return jnp.clip(values, -reach, reach).astype(kind)


def setup_inputs(seed: int = 0) -> dict:
    streams_of = jax.random.split(jax.random.key(seed), 6)
    near_blocks = centred(streams_of[0], (BOXES, NEAR, LEAF, LEAF), LEAF ** -0.5, 0.375, ((0, 128), (1, 4)))
    self_block = draw_self_block(jax.random.fold_in(streams_of[5], 71), 0)
    basis = centred(streams_of[2], (BOXES, LEAF, LEAF), (LEAF // 16) ** -0.5, 1.5, ((0, 128), (1, 4)))
    neighbours = draw_neighbours(jax.random.fold_in(streams_of[5], 71), 0)
    counts = touch_ends(jax.random.randint(streams_of[4], (BOXES,), LEAF // 2, LEAF + 1), jax.random.fold_in(streams_of[4], 1), LEAF // 2, LEAF).astype(jnp.int32)
    return {"near_blocks": near_blocks, "self_block": self_block, "basis": basis, "neighbours": neighbours, "counts": counts}


def solve_block(summed):
    corner = summed[:RED, :RED]
    side = summed[RED:, :RED]
    lower = jnp.linalg.cholesky(corner)
    solved = jax.scipy.linalg.cho_solve((lower, True), side.T)
    return solved.T

def reference(near_blocks, self_block, basis, neighbours, counts):
    positions = jnp.arange(LEAF, dtype=jnp.int32)
    keep_cols = positions[None, :] < counts[:, None]
    zero_value = jnp.zeros((), jnp.bfloat16)
    masked_basis = jnp.where(keep_cols[:, :, None], basis, zero_value)
    identity = positions[:, None] == positions[None, :]

    def one_box(inputs):
        blocks, self_rows, own_basis, own_masked, near_ids, keep_own = inputs
        both_kept = keep_own[:, None] & keep_own[None, :]
        diagonal_fill = jnp.where(identity & ~keep_own[:, None], jnp.ones((), jnp.bfloat16), zero_value)
        adjusted = jnp.where(both_kept, self_rows, diagonal_fill)
        product = jnp.dot(adjusted.astype(jnp.float32), own_basis.astype(jnp.float32), preferred_element_type=jnp.float32).astype(jnp.bfloat16)
        summed = jnp.dot(own_basis.T.astype(jnp.float32), product.astype(jnp.float32), preferred_element_type=jnp.float32)
        factor = solve_block(summed)
        near_basis = masked_basis[jnp.maximum(near_ids, 0)]
        near_work = jnp.einsum('krc,kcs->krs', blocks.astype(jnp.float32), near_basis.astype(jnp.float32))
        near_work = jnp.where(keep_own[None, :, None], near_work, 0.0).astype(jnp.bfloat16)
        projected = jnp.einsum('ck,jcs->jks', own_masked.astype(jnp.float32), near_work.astype(jnp.float32))
        update = jnp.einsum('ij,kjs->kis', factor, projected[:, :RED, :], precision=lax.Precision.HIGHEST)
        result = projected[:, RED:, :] - update
        result = jnp.where((near_ids >= 0)[:, None, None], result, 0.0)
        return result.astype(jnp.bfloat16)
    return lax.map(one_box, (near_blocks, self_block, basis, masked_basis, neighbours, keep_cols))
```

```python
import jax
import jax.numpy as jnp
from jax import lax
from jax.experimental import pallas as pl
from jax.experimental.pallas import tpu as pltpu
from jax.sharding import PartitionSpec as P

MESH = pl.DeviceIdType.MESH
F32 = jnp.float32
BF16 = jnp.bfloat16
HOPS = 3
BOX_DEV = 4
LVL = 4
LEAF = 256
RED = 128
PIECE = LEAF // LVL
SLOTS = 6
WINDOW = (2 * HOPS + 1) * BOX_DEV
PANEL = 32
N_COPY = 64


def matmul(a, b, dims=((1,), (0,)), precision=None):
    return lax.dot_general(a, b, (dims, ((), ())), precision=precision, preferred_element_type=F32)


def row_of(tile, j):
    return jnp.broadcast_to(tile[j : j + 1, :], tile.shape)


def lane_of(tile, c):
    return jnp.broadcast_to(tile[:, c : c + 1], tile.shape)


def eliminate_group(left, right, group, lane):
    tile_rows = lax.broadcasted_iota(jnp.int32, (8, RED), 0)
    others = [h for h in range(len(left)) if h != group]
    cols = [lane_of(left[group], lane + k) for k in range(8)]
    other_cols = {h: [lane_of(left[h], lane + k) for k in range(8)] for h in others}
    own_left, own_right = left[group], right[group]
    for j in range(0, 8, 2):
        first = {k: row_of(cols[k], j) for k in range(j, 8)}
        second = {k: row_of(cols[k], j + 1) for k in range(j, 8)}
        a, b, c, d = first[j], first[j + 1], second[j], second[j + 1]
        scale = 1.0 / (a * d - b * c)
        u = jnp.where(tile_rows == j, a - 1.0, jnp.where(tile_rows == j + 1, c, cols[j]))
        v = jnp.where(tile_rows == j, b, jnp.where(tile_rows == j + 1, d - 1.0, cols[j + 1]))
        m1 = (u * d - v * c) * scale
        m2 = (v * a - u * b) * scale
        for k in range(j + 2, 8):
            cols[k] = cols[k] - m1 * first[k] - m2 * second[k]
        own_left = own_left - m1 * row_of(own_left, j) - m2 * row_of(own_left, j + 1)
        own_right = own_right - m1 * row_of(own_right, j) - m2 * row_of(own_right, j + 1)
    left[group], right[group] = own_left, own_right
    rows_left = [row_of(own_left, k) for k in range(8)]
    rows_right = [row_of(own_right, k) for k in range(8)]
    for h in others:
        for k in range(8):
            left[h] = left[h] - other_cols[h][k] * rows_left[k]
            right[h] = right[h] - other_cols[h][k] * rows_right[k]


def eliminate_panel(system, panel):
    start = panel * PANEL
    groups = PANEL // 8
    left = [system[start + 8 * g : start + 8 * g + 8, :RED] for g in range(groups)]
    right = [system[start + 8 * g : start + 8 * g + 8, RED:] for g in range(groups)]
    for g in range(groups):
        eliminate_group(left, right, g, start + 8 * g)
    done = jnp.concatenate([jnp.concatenate(left, 0), jnp.concatenate(right, 0)], 1)
    cols = system[:, start : start + PANEL]
    system[...] = system[...] - matmul(cols, done, precision=lax.Precision.HIGHEST)
    system[start : start + PANEL, :] = done


def kernel(
    near_hbm, self_hbm, basis_hbm, nbr_ref, cnt_ref, out_ref,
    raw, win, self_rows, wt, near, work, system, send_sem, recv_sem, load_sem,
):
    b = lax.axis_index("box")
    y = lax.axis_index("lvl")
    boxes = lax.axis_size("box")
    side = 1 - 2 * lax.rem(b, 2)
    up, down, far = lax.rem(y + 1, LVL), lax.rem(y + 3, LVL), lax.rem(y + 2, LVL)
    ahead, behind = lax.rem(b + 2, boxes), lax.rem(b + boxes - 2, boxes)
    sibling, cross = b + side, lax.rem(b - side + boxes, boxes)

    def rows(level):
        return pl.ds(pl.multiple_of(level * PIECE, PIECE), PIECE)

    def slot(offset):
        return BOX_DEV * (offset + HOPS)

    loads = [
        pltpu.make_async_copy(basis_hbm, raw.at[:, rows(y)], load_sem.at[0]),
        pltpu.make_async_copy(self_hbm.at[y], self_rows.at[rows(y)], load_sem.at[1]),
        pltpu.make_async_copy(near_hbm, near, load_sem.at[2]),
    ]
    loads[0].start()
    loads[1].start()

    partners = [(b, up), (b, down), (b, far), (ahead, y), (behind, y), (sibling, y), (cross, y)]
    barrier = pltpu.get_barrier_semaphore()
    for partner in partners:
        pl.semaphore_signal(barrier, inc=1, device_id=partner, device_id_type=MESH)
    pl.semaphore_wait(barrier, len(partners))

    copies = []

    def send(source, target, device):
        k = len(copies)
        copy = pltpu.make_async_remote_copy(
            src_ref=source, dst_ref=target, send_sem=send_sem.at[k], recv_sem=recv_sem.at[k],
            device_id=device, device_id_type=MESH,
        )
        copy.start()
        copies.append(copy)
        return copy

    def wait(group):
        for copy in group:
            copy.wait_recv()

    first = []
    for level in (up, down, far):
        first.append(send(self_hbm.at[level], self_rows.at[rows(y)], (b, level)))
        first.append(send(basis_hbm.at[level], raw.at[level, rows(y)], (b, level)))

    def mask_rows(level):
        row_ids = level * PIECE + lax.broadcasted_iota(jnp.int32, (PIECE, LEAF), 0)
        for j in range(BOX_DEV):
            values = raw[j, rows(level), :].astype(F32)
            values = jnp.where(row_ids < cnt_ref[j], values, 0.0)
            win[slot(0) + j, rows(level), :] = values.astype(BF16)

    def to_ahead_and_behind(level):
        source = win.at[pl.ds(slot(0), BOX_DEV), rows(level)]
        return [
            send(source, win.at[pl.ds(slot(-2), BOX_DEV), rows(level)], (ahead, y)),
            send(source, win.at[pl.ds(slot(2), BOX_DEV), rows(level)], (behind, y)),
        ]

    def to_sibling(offset, level):
        source = win.at[pl.ds(slot(offset), BOX_DEV), rows(level)]
        return send(source, win.at[pl.ds(slot(offset - side), BOX_DEV), rows(level)], (sibling, y))

    def to_cross(level):
        source = win.at[pl.ds(slot(2 * side), BOX_DEV), rows(level)]
        return send(source, win.at[pl.ds(slot(3 * side), BOX_DEV), rows(level)], (cross, y))

    def around(offset):
        upward = win.at[pl.ds(slot(offset), 2), rows(down)]
        downward = win.at[pl.ds(slot(offset) + 2, 2), rows(up)]
        return [send(upward, upward, (b, up)), send(downward, downward, (b, down))]

    loads[0].wait()
    mask_rows(y)
    z_own = to_ahead_and_behind(y)
    rest_down, rest_up = [], []
    for k in range(1, BOX_DEV):
        j, i = lax.rem(up + k, BOX_DEV), lax.rem(down + k, BOX_DEV)
        rest_down.append(send(raw.at[j, rows(y)], raw.at[j, rows(y)], (b, up)))
        rest_up.append(send(raw.at[i, rows(y)], raw.at[i, rows(y)], (b, down)))
    shared = [to_sibling(0, y)]
    loads[2].start()

    wait(first)
    loads[1].wait()
    own_count = cnt_ref[y]
    row_ids = lax.broadcasted_iota(jnp.int32, (LEAF, LEAF), 0)
    col_ids = lax.broadcasted_iota(jnp.int32, (LEAF, LEAF), 1)
    kept = (row_ids < own_count) & (col_ids < own_count)
    unit = jnp.where((row_ids == col_ids) & (row_ids >= own_count), 1.0, 0.0)
    adjusted = jnp.where(kept, self_rows[...].astype(F32), unit).astype(BF16)
    own_basis = raw[y]
    product = matmul(adjusted, own_basis[:, :RED]).astype(BF16)
    total = matmul(product, own_basis, ((0,), (0,)))
    corner = total[:, :RED]
    corner = (corner + corner.T) * 0.5
    diagonal = jnp.where(row_ids[:RED, :RED] == col_ids[:RED, :RED], corner, 0.0)
    scale_rows = lax.rsqrt(jnp.sum(diagonal, axis=1, keepdims=True))
    scale_cols = lax.rsqrt(jnp.sum(diagonal, axis=0, keepdims=True))
    system[:, :RED] = corner * scale_rows * scale_cols
    system[:, RED:] = total[:, RED:] * scale_rows

    wait(rest_down)
    mask_rows(down)
    z_down = to_ahead_and_behind(down)
    wait(rest_up)
    mask_rows(up)
    z_up = to_ahead_and_behind(up)
    far_rows = []
    for j in (lax.rem(up + 1, BOX_DEV), lax.rem(up + 2, BOX_DEV)):
        far_rows.append(send(raw.at[j, rows(down)], raw.at[j, rows(down)], (b, up)))
    j = lax.rem(down + 3, BOX_DEV)
    far_rows.append(send(raw.at[j, rows(up)], raw.at[j, rows(up)], (b, down)))
    shared += [to_sibling(0, down), to_sibling(0, up)]

    eliminate_panel(system, 0)

    wait(z_own)
    crossed = [to_cross(y)]
    shared += [to_sibling(2, y), to_sibling(-2, y)]

    eliminate_panel(system, 1)

    wait(z_down)
    crossed.append(to_cross(down))
    wait(z_up)
    crossed.append(to_cross(up))
    rounds = around(2) + around(-2)
    for level in (down, up):
        shared += [to_sibling(2, level), to_sibling(-2, level)]
    wait(far_rows)
    mask_rows(far)
    shared.append(to_sibling(0, far))

    eliminate_panel(system, 2)

    wait(crossed)
    odd = around(-3 * side)
    wait(rounds)
    shared += [to_sibling(2, far), to_sibling(-2, far)]

    eliminate_panel(system, 3)

    solved = system[:, RED:] * scale_rows
    identity = jnp.where(row_ids[:RED, :RED] == col_ids[:RED, :RED], 1.0, 0.0)
    both = jnp.concatenate([-solved, identity], axis=0)
    own_masked = win[slot(0) + y].astype(F32)
    wt[y] = matmul(both, own_masked, ((0,), (1,)), lax.Precision.HIGHEST).astype(BF16)
    factors = [send(wt.at[y], wt.at[y], (b, level)) for level in (up, down, far)]

    wait(odd)
    wait(shared)
    loads[2].wait()
    first_box = BOX_DEV * (b - HOPS)

    def multiply(k, carry):
        for i in range(BOX_DEV):
            box = nbr_ref[i, k]
            place = jnp.clip(box - first_box, 0, WINDOW - 1)
            work[i, k] = matmul(near[i, k], win[place]).astype(BF16)
        return carry

    lax.fori_loop(0, SLOTS, multiply, 0)

    wait(factors)

    def project(k, carry):
        for i in range(BOX_DEV):
            used = nbr_ref[i, k] >= 0
            value = matmul(wt[i], work[i, k])
            out_ref[i, k] = jnp.where(used, value, 0.0).astype(BF16)
        return carry

    lax.fori_loop(0, SLOTS, project, 0)

    for copy in copies:
        copy.wait_send()


def local(near_blocks, self_block, basis, neighbours, counts):
    anywhere = pl.BlockSpec(memory_space=pl.ANY)
    scalars = pl.BlockSpec(memory_space=pltpu.SMEM)
    return pl.pallas_call(
        kernel,
        out_shape=jax.ShapeDtypeStruct((BOX_DEV, SLOTS, RED, LEAF), BF16),
        in_specs=[anywhere, anywhere, anywhere, scalars, scalars],
        out_specs=pl.BlockSpec(memory_space=pltpu.VMEM),
        scratch_shapes=[
            pltpu.VMEM((BOX_DEV, LEAF, LEAF), BF16),
            pltpu.VMEM((WINDOW, LEAF, LEAF), BF16),
            pltpu.VMEM((LEAF, LEAF), BF16),
            pltpu.VMEM((BOX_DEV, RED, LEAF), BF16),
            pltpu.VMEM((BOX_DEV, SLOTS, LEAF, LEAF), BF16),
            pltpu.VMEM((BOX_DEV, SLOTS, LEAF, LEAF), BF16),
            pltpu.VMEM((RED, LEAF), F32),
            pltpu.SemaphoreType.DMA((N_COPY,)),
            pltpu.SemaphoreType.DMA((N_COPY,)),
            pltpu.SemaphoreType.DMA((3,)),
        ],
        compiler_params=pltpu.CompilerParams(
            collective_id=0, has_side_effects=True, vmem_limit_bytes=40 * 2**20
        ),
        cost_estimate=pl.CostEstimate(flops=1_300_000_000, bytes_accessed=5_000_000, transcendentals=0),
        name="eliminate_level",
    )(near_blocks, self_block, basis, neighbours, counts)


def solution(mesh):
    return jax.shard_map(
        local,
        mesh=mesh,
        in_specs=(
            P("box", "lvl", None, None),
            P("box", "lvl", None),
            P("box", "lvl", None),
            P("box", "lvl"),
            P("box"),
        ),
        out_specs=P("box", "lvl", None, None),
        check_vma=False,
    )
```

```python
import jax
import jax.numpy as jnp
from jax import lax
from jax.experimental import pallas as pl
from jax.experimental.pallas import tpu as pltpu
from jax.sharding import PartitionSpec as P

MESH = pl.DeviceIdType.MESH
F32 = jnp.float32
BF16 = jnp.bfloat16
HOPS = 3
BOX_DEV = 4
LVL = 4
LEAF = 256
RED = 128
PIECE = LEAF // LVL
SLOTS = 6
WINDOW = (2 * HOPS + 1) * BOX_DEV
PANEL = 32
Z_BOXES = 32
N_COPY = 96
SELF, RAW, FACTOR, SHARE, TO, ON, ALL = range(100, 107)
LOW, HIGH, ODD_LOW, ODD_HIGH = range(200, 204)
OWN, UP, DOWN, FAR = range(300, 304)
ACROSS = {LOW: HIGH, HIGH: LOW, ODD_LOW: ODD_HIGH, ODD_HIGH: ODD_LOW}


def matmul(a, b, dims=((1,), (0,)), precision=None):
    return lax.dot_general(a, b, (dims, ((), ())), precision=precision, preferred_element_type=F32)


def row_of(tile, j):
    return jnp.broadcast_to(tile[j : j + 1, :], tile.shape)


def lane_of(tile, c):
    return jnp.broadcast_to(tile[:, c : c + 1], tile.shape)


def eliminate_group(left, right, group, lane):
    tile_rows = lax.broadcasted_iota(jnp.int32, (8, RED), 0)
    others = [h for h in range(len(left)) if h != group]
    cols = [lane_of(left[group], lane + k) for k in range(8)]
    other_cols = {h: [lane_of(left[h], lane + k) for k in range(8)] for h in others}
    own_left, own_right = left[group], right[group]
    for j in range(0, 8, 2):
        first = {k: row_of(cols[k], j) for k in range(j, 8)}
        second = {k: row_of(cols[k], j + 1) for k in range(j, 8)}
        a, b, c, d = first[j], first[j + 1], second[j], second[j + 1]
        scale = 1.0 / (a * d - b * c)
        u = jnp.where(tile_rows == j, a - 1.0, jnp.where(tile_rows == j + 1, c, cols[j]))
        v = jnp.where(tile_rows == j, b, jnp.where(tile_rows == j + 1, d - 1.0, cols[j + 1]))
        m1 = (u * d - v * c) * scale
        m2 = (v * a - u * b) * scale
        for k in range(j + 2, 8):
            cols[k] = cols[k] - m1 * first[k] - m2 * second[k]
        own_left = own_left - m1 * row_of(own_left, j) - m2 * row_of(own_left, j + 1)
        own_right = own_right - m1 * row_of(own_right, j) - m2 * row_of(own_right, j + 1)
    left[group], right[group] = own_left, own_right
    rows_left = [row_of(own_left, k) for k in range(8)]
    rows_right = [row_of(own_right, k) for k in range(8)]
    for h in others:
        for k in range(8):
            left[h] = left[h] - other_cols[h][k] * rows_left[k]
            right[h] = right[h] - other_cols[h][k] * rows_right[k]


def eliminate_panel(system, panel):
    start = panel * PANEL
    groups = PANEL // 8
    left = [system[start + 8 * g : start + 8 * g + 8, :RED] for g in range(groups)]
    right = [system[start + 8 * g : start + 8 * g + 8, RED:] for g in range(groups)]
    for g in range(groups):
        eliminate_group(left, right, g, start + 8 * g)
    done = jnp.concatenate([jnp.concatenate(left, 0), jnp.concatenate(right, 0)], 1)
    cols = system[:, start : start + PANEL]
    system[...] = system[...] - matmul(cols, done, precision=lax.Precision.HIGHEST)
    system[start : start + PANEL, :] = done


def kernel(
    near_hbm, self_hbm, basis_hbm, nbr_hbm, cnt_hbm, out_ref,
    raw, win, self_rows, factors, wt, near_ref, work, system, nbr_ref, cnt_ref, fill,
    send_sem, recv_sem, load_sem, out_sem, low_sem, cross_sem,
):
    b = lax.axis_index("box")
    y = lax.axis_index("lvl")
    boxes = lax.axis_size("box")
    core = lax.rem(b, 2)
    side = 1 - 2 * core
    up, down, far = lax.rem(y + 1, LVL), lax.rem(y + 3, LVL), lax.rem(y + 2, LVL)
    levels = {UP: up, DOWN: down, FAR: far}
    sibling = b + side
    z_place = lax.rem(b, Z_BOXES)

    def split(guard, wraps):
        return guard, guard & jnp.logical_not(wraps), guard & wraps

    has_low, low_near, low_wrap = split(b >= 2, z_place < 2)
    has_high, high_near, high_wrap = split(b < boxes - 2, z_place >= Z_BOXES - 2)
    odd_low, odd_low_near, odd_low_wrap = split((core == 0) & (b >= 4), z_place < 4)
    odd_high, odd_high_near, odd_high_wrap = split((core == 1) & (b < boxes - 4), z_place >= Z_BOXES - 4)

    def rows(level):
        return pl.ds(pl.multiple_of(level * PIECE, PIECE), PIECE)

    def slot(offset):
        return BOX_DEV * (offset + HOPS)

    def piece(offset, level, first=0, count=BOX_DEV):
        return win.at[pl.ds(slot(offset) + first, count), rows(level)]

    loads = [
        pltpu.make_async_copy(basis_hbm, raw.at[:, rows(y)], load_sem.at[0]),
        pltpu.make_async_copy(self_hbm.at[y], self_rows.at[rows(y)], load_sem.at[1]),
        pltpu.make_async_copy(near_hbm, near_ref, load_sem.at[2]),
        pltpu.make_async_copy(cnt_hbm, cnt_ref, load_sem.at[3]),
        pltpu.make_async_copy(nbr_hbm, nbr_ref, load_sem.at[4]),
    ]
    for load in loads:
        load.start()

    barrier = pltpu.get_barrier_semaphore()

    def greet(device):
        pl.semaphore_signal(barrier, inc=1, device_id=device, device_id_type=MESH)

    for device in ((b, up), (b, down), (b, far), (sibling, y)):
        greet(device)
    pl.when(has_low)(lambda: greet((b - 2, y)))
    pl.when(odd_low)(lambda: greet((b - 3, y)))
    pl.semaphore_wait(barrier, 4 + has_high.astype(jnp.int32) + odd_high.astype(jnp.int32))

    def answer(semaphore, device):
        pl.semaphore_signal(semaphore, inc=1, device_id=device, device_id_type=MESH)

    pl.when(has_high)(lambda: answer(low_sem, (b + 2, y)))
    pl.when(odd_high)(lambda: answer(cross_sem, (b + 3, y)))

    plans = {}

    def plan(name, source, target, device, guard=None):
        k = len(plans)
        copy = pltpu.make_async_remote_copy(
            src_ref=source, dst_ref=target, send_sem=send_sem.at[k], recv_sem=recv_sem.at[k],
            device_id=device, device_id_type=MESH,
        )
        plans[name] = (copy, guard)

    def go(*names):
        for name in names:
            plans[name][0].start()

    def got(*names):
        for name in names:
            plans[name][0].wait_recv()

    for way, level in levels.items():
        plan((SELF, way), self_hbm.at[level], self_rows.at[rows(y)], (b, level))
        plan((FACTOR, way), factors.at[y], factors.at[y], (b, level))
    for way, level in ((UP, up), (DOWN, down)):
        plan((RAW, way), basis_hbm, raw.at[:, rows(y)], (b, level))
    plan((RAW, FAR), basis_hbm.at[far], raw.at[far, rows(y)], (b, far))
    for k in range(1, BOX_DEV):
        level, source = (up, down) if k < 3 else (down, up)
        j = lax.rem(level + k, BOX_DEV)
        plan((RAW, k, ON), raw.at[j, rows(source)], raw.at[j, rows(source)], (b, level))
    for name, offset, near_guard, wrap_guard in (
        (LOW, -2, low_near, low_wrap), (HIGH, 2, high_near, high_wrap),
        (ODD_LOW, -3, odd_low_near, odd_low_wrap), (ODD_HIGH, 3, odd_high_near, odd_high_wrap),
    ):
        for way, first, level in ((DOWN, 0, down), (UP, 2, up)):
            plan((name, OWN, way), piece(offset, y, first, 2), piece(offset, y, first, 2), (b, level), near_guard)
        for way, first, level, source in ((UP, 0, up, down), (DOWN, 2, down, up)):
            half = piece(offset, source, first, 2)
            plan((name, FAR, way), half, half, (b, level), near_guard)
        for way, level in ((UP, up), (DOWN, down)):
            plan((name, ALL, way), piece(offset, y), piece(offset, y), (b, level), wrap_guard)
    for name, offset, device, guard, near_guard, wrap_guard in (
        (LOW, 2, b - 2, has_low, low_near, low_wrap),
        (HIGH, -2, b + 2, has_high, high_near, high_wrap),
        (ODD_LOW, 3, b - 3, odd_low, odd_low_near, odd_low_wrap),
        (ODD_HIGH, -3, b + 3, odd_high, odd_high_near, odd_high_wrap),
    ):
        plan((TO, name, OWN), piece(0, y), piece(offset, y), (device, y), guard)
        plan((TO, name, FAR), piece(0, far), piece(offset, far), (device, y), wrap_guard)
        for way, first, level in ((DOWN, 0, down), (UP, 2, up)):
            plan((TO, name, way), piece(0, level, first, 2), piece(offset, level, first, 2), (device, y), near_guard)

    def plan_share(name, offset, level, guard, first=0, count=BOX_DEV):
        target = piece(offset - side, level, first, count)
        plan((SHARE, offset, *name), piece(offset, level, first, count), target, (sibling, y), guard)

    for way, level in ((OWN, y), (UP, up), (DOWN, down), (FAR, far)):
        plan_share((way,), 0, level, None)
    for offset, guard, near_guard, wrap_guard in ((-2, has_low, low_near, low_wrap), (2, has_high, high_near, high_wrap)):
        plan_share((OWN,), offset, y, guard)
        for way, level in levels.items():
            plan_share((ALL, way), offset, level, wrap_guard)
            plan_share((way, 0), offset, level, near_guard, 0, 2)
            plan_share((way, 2), offset, level, near_guard, 2, 2)

    def mask_rows(level):
        row_ids = level * PIECE + lax.broadcasted_iota(jnp.int32, (PIECE, LEAF), 0)
        for j in range(BOX_DEV):
            values = raw[j, rows(level), :].astype(F32)
            values = jnp.where(row_ids < cnt_ref[j], values, 0.0)
            win[slot(0) + j, rows(level), :] = values.astype(BF16)

    loads[0].wait()
    loads[3].wait()
    mask_rows(y)
    pl.when(has_high)(lambda: go((TO, HIGH, OWN)))
    go((RAW, UP), (RAW, DOWN))
    pl.when(odd_high)(lambda: go((TO, ODD_HIGH, OWN)))

    def to_low():
        pl.semaphore_wait(low_sem, 1)
        go((TO, LOW, OWN))

    def to_odd_low():
        pl.semaphore_wait(cross_sem, 1)
        go((TO, ODD_LOW, OWN))

    pl.when(low_near)(to_low)
    pl.when(odd_low_near)(to_odd_low)
    for way in levels:
        go((SELF, way))
    go((RAW, FAR), (SHARE, 0, OWN))

    def onward(way, *names):
        guards = {HIGH: high_near, LOW: low_near, ODD_HIGH: odd_high_near, ODD_LOW: odd_low_near}
        for name in names:
            pl.when(guards[name])(lambda name=name: go((TO, name, way)))

    got((RAW, UP))
    go((RAW, 1, ON), (RAW, 2, ON))
    mask_rows(down)
    onward(DOWN, HIGH, LOW)
    got((RAW, DOWN))
    go((RAW, 3, ON))
    mask_rows(up)
    onward(UP, HIGH, LOW, ODD_HIGH, ODD_LOW)
    onward(DOWN, ODD_HIGH, ODD_LOW)
    go((SHARE, 0, DOWN), (SHARE, 0, UP))

    got((SELF, UP), (SELF, DOWN), (SELF, FAR), (RAW, FAR))
    loads[1].wait()
    own_count = cnt_ref[y]
    row_ids = lax.broadcasted_iota(jnp.int32, (LEAF, LEAF), 0)
    col_ids = lax.broadcasted_iota(jnp.int32, (LEAF, LEAF), 1)
    kept = (row_ids < own_count) & (col_ids < own_count)
    unit = jnp.where((row_ids == col_ids) & (row_ids >= own_count), 1.0, 0.0)
    adjusted = jnp.where(kept, self_rows[...].astype(F32), unit).astype(BF16)
    own_basis = raw[y]
    product = matmul(adjusted, own_basis[:, :RED]).astype(BF16)
    total = matmul(product, own_basis, ((0,), (0,)))
    corner = total[:, :RED]
    corner = (corner + corner.T) * 0.5
    diagonal = jnp.where(row_ids[:RED, :RED] == col_ids[:RED, :RED], corner, 0.0)
    scale_rows = lax.rsqrt(jnp.sum(diagonal, axis=1, keepdims=True))
    scale_cols = lax.rsqrt(jnp.sum(diagonal, axis=0, keepdims=True))
    system[:, :RED] = corner * scale_rows * scale_cols
    system[:, RED:] = total[:, RED:] * scale_rows

    eliminate_panel(system, 0)

    shared = {LOW: -2, HIGH: 2}

    def arrived(name, way, parts, share):
        def step():
            got((TO, ACROSS[name], way))
            go(*[(name, *part) for part in parts])
            if name in shared:
                go((SHARE, shared[name], *share))

        return step

    near = ((LOW, low_near), (HIGH, high_near), (ODD_LOW, odd_low_near), (ODD_HIGH, odd_high_near))
    wrap = ((LOW, low_wrap), (HIGH, high_wrap), (ODD_LOW, odd_low_wrap), (ODD_HIGH, odd_high_wrap))
    for name, guard in near:
        pl.when(guard)(arrived(name, OWN, [(OWN, DOWN), (OWN, UP)], (OWN,)))
    for k in range(1, BOX_DEV):
        got((RAW, k, ON))
    mask_rows(far)
    pl.when(high_wrap)(lambda: go((TO, HIGH, FAR)))
    pl.when(odd_high_wrap)(lambda: go((TO, ODD_HIGH, FAR)))
    go((SHARE, 0, FAR))

    eliminate_panel(system, 1)

    pl.when(low_wrap)(to_low)
    pl.when(odd_low_wrap)(to_odd_low)
    pl.when(low_wrap)(lambda: go((TO, LOW, FAR)))
    pl.when(odd_low_wrap)(lambda: go((TO, ODD_LOW, FAR)))


    eliminate_panel(system, 2)
    eliminate_panel(system, 3)

    factors[y] = (system[:, RED:] * scale_rows).T.astype(BF16)
    go((FACTOR, UP), (FACTOR, DOWN), (FACTOR, FAR))

    for name, guard in (wrap[1], wrap[3]):
        pl.when(guard)(arrived(name, OWN, [(ALL, UP), (ALL, DOWN)], (OWN,)))
    for way, parts, share in ((DOWN, [(FAR, UP)], (DOWN, 0)), (UP, [(FAR, DOWN)], (UP, 2))):
        for name, guard in near:
            pl.when(guard)(arrived(name, way, parts, share))
    for name, guard in (wrap[0], wrap[2]):
        pl.when(guard)(arrived(name, OWN, [(ALL, UP), (ALL, DOWN)], (OWN,)))

    def passed_on(name, parts):
        def step():
            for part, way in parts:
                got((name, *part))
                if name in shared:
                    go((SHARE, shared[name], *way))

        return step

    for name, guard in near:
        pl.when(guard)(passed_on(name, [((OWN, DOWN), (UP, 0)), ((OWN, UP), (DOWN, 2))]))

    got((FACTOR, UP), (FACTOR, DOWN), (FACTOR, FAR))
    unit = jnp.where(row_ids[:RED, :RED] == col_ids[:RED, :RED], 1.0, 0.0)
    for i in range(BOX_DEV):
        both = jnp.concatenate([-factors[i].astype(F32), unit], axis=1).astype(BF16)
        wt[i] = matmul(both, win[slot(0) + i], ((1,), (1,))).astype(BF16)
    loads[2].wait()
    loads[4].wait()

    def transform(k, carry):
        for i in range(BOX_DEV):
            work[i, k] = matmul(wt[i], near_ref[i, k]).astype(BF16)
        return carry

    lax.fori_loop(0, SLOTS, transform, 0)

    for name, guard in near:
        pl.when(guard)(passed_on(name, [((FAR, UP), (FAR, 0)), ((FAR, DOWN), (FAR, 2))]))
    for name, guard in wrap:
        pl.when(guard)(passed_on(name, [((ALL, UP), (ALL, DOWN)), ((ALL, DOWN), (ALL, UP))]))
        pl.when(guard)(arrived(name, FAR, [], (ALL, FAR)))
    got((SHARE, 0, OWN), (SHARE, 0, UP), (SHARE, 0, DOWN), (SHARE, 0, FAR))
    for offset, guard, near_guard, wrap_guard in ((-2, has_low, low_near, low_wrap), (2, has_high, high_near, high_wrap)):
        halves = [(SHARE, offset, way, first) for way in levels for first in (0, 2)]
        wholes = [(SHARE, offset, ALL, way) for way in levels]
        pl.when(guard)(lambda offset=offset: got((SHARE, offset, OWN)))
        pl.when(near_guard)(lambda names=halves: got(*names))
        pl.when(wrap_guard)(lambda names=wholes: got(*names))
    first_box = BOX_DEV * (b - HOPS)

    def stored(k, i):
        return pltpu.make_async_copy(fill.at[k, i], out_ref.at[i, k], out_sem.at[k, i])

    def finish(k, carry):
        for i in range(BOX_DEV):
            box = nbr_ref[i, k]
            place = jnp.clip(box - first_box, 0, WINDOW - 1)
            value = matmul(work[i, k], win[place])
            fill[k, i] = jnp.where(box >= 0, value, 0.0).astype(BF16)
        for i in range(BOX_DEV):
            stored(k, i).start()
        return carry

    lax.fori_loop(0, SLOTS, finish, 0)
    for k in range(SLOTS):
        for i in range(BOX_DEV):
            stored(k, i).wait()

    for copy, guard in plans.values():
        if guard is None:
            copy.wait_send()
        else:
            pl.when(guard)(copy.wait_send)


def local(near_blocks, self_block, basis, neighbours, counts):
    anywhere = pl.BlockSpec(memory_space=pltpu.HBM)
    return pl.pallas_call(
        kernel,
        out_shape=jax.ShapeDtypeStruct((BOX_DEV, SLOTS, RED, LEAF), BF16),
        in_specs=[anywhere] * 5,
        out_specs=anywhere,
        scratch_shapes=[
            pltpu.VMEM((BOX_DEV, LEAF, LEAF), BF16),
            pltpu.VMEM((WINDOW, LEAF, LEAF), BF16),
            pltpu.VMEM((LEAF, LEAF), BF16),
            pltpu.VMEM((BOX_DEV, RED, RED), BF16),
            pltpu.VMEM((BOX_DEV, RED, LEAF), BF16),
            pltpu.VMEM((BOX_DEV, SLOTS, LEAF, LEAF), BF16),
            pltpu.VMEM((BOX_DEV, SLOTS, RED, LEAF), BF16),
            pltpu.VMEM((RED, LEAF), F32),
            pltpu.SMEM((BOX_DEV, SLOTS), jnp.int32),
            pltpu.SMEM((BOX_DEV,), jnp.int32),
            pltpu.VMEM((SLOTS, BOX_DEV, RED, LEAF), BF16),
            pltpu.SemaphoreType.DMA((N_COPY,)),
            pltpu.SemaphoreType.DMA((N_COPY,)),
            pltpu.SemaphoreType.DMA((5,)),
            pltpu.SemaphoreType.DMA((SLOTS, BOX_DEV)),
            pltpu.SemaphoreType.REGULAR,
            pltpu.SemaphoreType.REGULAR,
        ],
        compiler_params=pltpu.CompilerParams(
            collective_id=0, has_side_effects=True, vmem_limit_bytes=59 * 2**20
        ),
        cost_estimate=pl.CostEstimate(flops=1_300_000_000, bytes_accessed=5_000_000, transcendentals=0),
        name="eliminate_level",
    )(near_blocks, self_block, basis, neighbours, counts)


def solution(mesh):
    return jax.shard_map(
        local,
        mesh=mesh,
        in_specs=(
            P("box", "lvl", None, None),
            P("box", "lvl", None),
            P("box", "lvl", None),
            P("box", "lvl"),
            P("box"),
        ),
        out_specs=P("box", "lvl", None, None),
        check_vma=False,
    )
```
